32 devices in a mesh: group: 2 (over y), row: 16 (over z, x, core).
Axes of the slice: x: 2, y: 2, z: 4, core: 2. Of those that a mesh axis runs over, the one named last changes fastest.
Arguments:
- x_first: bfloat16 [16384, 384], P('row', 'group'), parts along dimension 1, may hold values from -6 to 6
- x_layer: bfloat16 [24576, 384], P('row', 'group'), parts along dimension 1, may hold values from -6 to 6
- upstream: bfloat16 [16384, 384], P('row', 'group'), parts along dimension 1, may hold values from -4 to 4
- weight: bfloat16 [16384, 24576], P('row'), may hold values from -0.0546875 to 0.0546875
- bias: float32 [16384], P('row'), may hold values from -6 to 6
Outputs:
- first_grad: bfloat16 [16384, 384], P('row', 'group'), parts along dimension 1
- layer_grad: bfloat16 [24576, 384], P('row', 'group'), parts along dimension 1
- weight_grad: bfloat16 [32768, 24576], P(('group', 'row')), parts along dimension 0
- bias_grad: float32 [32768], P(('group', 'row')), parts along dimension 0
The draws below stay inside these ranges and needn't reach their ends.
There are 2 independent parts, one for each index of `group`. The reference program is written for one: setup_inputs(seed, part) draws one part's arguments, and reference() takes and returns one part's arrays. A program takes and returns all parts, laid end to end along the dimension named above; an argument that names none is the same for every part. Nothing has to cross between parts.
All inputs are finite; a program needn't handle non-finite values.
Results may differ from the reference program's by a relative error of at most 0.005.
Values may be sent and summed in bfloat16 or wider, within the bound.
A program may use at most 256 MiB of HBM per device.

```python
import jax
import jax.numpy as jnp
from jax import lax

IN = 24576
OUT = 16384
SAMPLES = 192
N_ROW = 16


def raised(result, stream_key, source, target, blocks, factor):
    def block_of(dim):
        return (jnp.arange(result.shape[dim]) // (result.shape[dim] // blocks)).reshape((-1,) + (1,) * (result.ndim - 1 - dim))

    near = jax.random.permutation(stream_key, blocks)[block_of(target)]
    other_side = (block_of(target) + blocks // 2) % blocks
    return jnp.where((block_of(source) == near) | (block_of(source) == other_side), factor * result, result)


def block_levels(own_key, dims, shards, least, largest):
    level, own = 1.0, jax.random.fold_in(own_key, 6)
    for axis_at, blocks in shards:
        steps = jnp.exp(jax.random.uniform(jax.random.fold_in(own, axis_at), (blocks,), jnp.float32, least / len(shards), largest / len(shards)))
        level = level * jnp.repeat(steps, dims[axis_at] // blocks).reshape([-1 if axis == axis_at else 1 for axis in range(len(dims))])
    return level


def noise(rng, extent, deviation, limit, pieces=(), kind=jnp.bfloat16):
    entries = deviation * jax.random.normal(rng, extent, jnp.float32)
    if pieces:
        entries = entries * block_levels(rng, extent, pieces, -0.22, 0.18)
    return jnp.clip(entries, -limit, limit).astype(kind)


def gaussian_with(key, shape, spread, limit, pieces, heavy, dtype=jnp.bfloat16):
    result = spread * jax.random.normal(key, shape, jnp.float32)
    if pieces:
        result = result * block_levels(key, shape, pieces, -0.22, 0.18)
    return jnp.clip(raised(result, jax.random.fold_in(key, 3), *heavy), -limit, limit).astype(dtype)


def setup_inputs(seed: int = 0, part: int = 0) -> dict:
    streams_of = jax.random.split(jax.random.key(seed), 6)
    part_keys = jax.random.split(jax.random.fold_in(streams_of[5], part), 6)
    x_first = noise(part_keys[0], (OUT, SAMPLES), 1.0, 6.0, ((0, 16),))
    x_layer = noise(part_keys[1], (IN, SAMPLES), 1.0, 6.0, ((0, 16),))
    upstream = noise(part_keys[2], (OUT, SAMPLES), 0.25, 4.0, ((0, 16),))
    weight = gaussian_with(streams_of[3], (OUT, IN), IN ** -0.5, 0.0546875, ((0, 16),), (0, 1, 16, 2.0))
    bias = noise(streams_of[4], (OUT,), 1.0, 6.0, ((0, 16),), jnp.float32)
    return {"x_first": x_first, "x_layer": x_layer, "upstream": upstream, "weight": weight, "bias": bias}


def reference(x_first, x_layer, upstream, weight, bias):
    affine = jnp.dot(weight, x_layer, preferred_element_type=jnp.float32) + bias[:, None]
    upstream_wide = upstream.astype(jnp.float32)
    first_grad = (upstream_wide * affine).astype(jnp.bfloat16)
    modulated = (upstream_wide * x_first.astype(jnp.float32)).astype(jnp.bfloat16)
    layer_grad = lax.dot_general(weight, modulated, (((0,), (0,)), ((), ())), preferred_element_type=jnp.float32).astype(jnp.bfloat16)
    blocks = modulated.reshape(N_ROW, OUT // N_ROW, SAMPLES)

    def block_grad(mod_block):
        return lax.dot_general(mod_block, x_layer, (((1,), (1,)), ((), ())), preferred_element_type=jnp.float32).astype(jnp.bfloat16)
    weight_grad = lax.map(block_grad, blocks).reshape(OUT, IN)
    bias_grad = lax.optimization_barrier(jnp.sum(modulated.astype(jnp.float32), axis=1))
    return (first_grad, layer_grad, weight_grad, bias_grad)
```

```python
import functools

import jax
import jax.numpy as jnp
from jax import lax
from jax.experimental import pallas as pl
from jax.experimental.pallas import tpu as pltpu
from jax.sharding import PartitionSpec as P

F32 = jnp.float32
BF16 = jnp.bfloat16


def ring_of(n):
    width = {8: 2, 64: 4}.get(n, 2)
    depth = n // width
    walk = []
    for z in range(depth):
        xs = list(range(1, width))
        walk += [z * width + x for x in (xs if z % 2 == 0 else xs[::-1])]
    return walk + [z * width for z in reversed(range(depth))]


def partial_kernel(parts, where, mod_t, w, away, own):
    t = pl.program_id(0)
    out = jnp.dot(mod_t[...], w[...], preferred_element_type=F32)

    @pl.when(t < parts)
    def _():
        away[...] = out.astype(away.dtype)

    @pl.when(t >= parts)
    def _():
        own[...] = out


def partials(where, mod_t, weight, block, parts):
    samples, rows = mod_t.shape
    tile = block // parts
    return pl.pallas_call(
        functools.partial(partial_kernel, parts),
        grid_spec=pltpu.PrefetchScalarGridSpec(
            num_scalar_prefetch=1,
            grid=(2 * parts,),
            in_specs=[
                pl.BlockSpec((samples, rows), lambda t, s: (0, 0)),
                pl.BlockSpec((rows, tile), lambda t, s: (0, jnp.where(t < parts, s[1] * parts + t, s[0] * parts + t - parts))),
            ],
            out_specs=[
                pl.BlockSpec((samples, tile), lambda t, s: (0, jnp.minimum(t, parts - 1))),
                pl.BlockSpec((samples, tile), lambda t, s: (0, jnp.maximum(t - parts, 0))),
            ],
        ),
        out_shape=[jax.ShapeDtypeStruct((samples, block), BF16), jax.ShapeDtypeStruct((samples, block), F32)],
        compiler_params=pltpu.CompilerParams(vmem_limit_bytes=24 << 20),
        cost_estimate=pl.CostEstimate(flops=4 * samples * rows * block, bytes_accessed=4 * rows * block, transcendentals=0),
    )(where, mod_t, weight)


def forward_kernel(parts, where, w, mod, xa, xb, total_in, grad_in, total, grad):
    t = pl.program_id(0)

    @pl.when(t == 0)
    def _():
        total[...] = total_in[...]

    def step(x):
        total[...] += lax.dot_general(w[...], x[...], (((1,), (1,)), ((), ())), preferred_element_type=F32)
        grad[...] = jnp.dot(mod[...], x[...], preferred_element_type=F32).astype(grad.dtype)

    pl.when(t < parts)(lambda: step(xa))
    pl.when(t >= parts)(lambda: step(xb))


def forward(where, weight, mod, xa, xb, total, grad, parts):
    rows, samples = mod.shape
    block = xa.shape[1]
    tile = block // parts

    def column(t, s):
        return (0, jnp.where(t < parts, s[0] * parts + t, s[1] * parts + t - parts))

    return pl.pallas_call(
        functools.partial(forward_kernel, parts),
        grid_spec=pltpu.PrefetchScalarGridSpec(
            num_scalar_prefetch=1,
            grid=(2 * parts,),
            in_specs=[
                pl.BlockSpec((rows, tile), column),
                pl.BlockSpec((rows, samples), lambda t, s: (0, 0)),
                pl.BlockSpec((samples, tile), lambda t, s: (0, jnp.minimum(t, parts - 1))),
                pl.BlockSpec((samples, tile), lambda t, s: (0, jnp.maximum(t - parts, 0))),
                pl.BlockSpec((rows, samples), lambda t, s: (0, 0)),
                pl.BlockSpec(memory_space=pl.ANY),
            ],
            out_specs=[
                pl.BlockSpec((rows, samples), lambda t, s: (0, 0)),
                pl.BlockSpec((rows, tile), column),
            ],
        ),
        out_shape=[jax.ShapeDtypeStruct(total.shape, F32), jax.ShapeDtypeStruct(grad.shape, BF16)],
        input_output_aliases={5: 0, 6: 1},
        compiler_params=pltpu.CompilerParams(vmem_limit_bytes=32 << 20),
        cost_estimate=pl.CostEstimate(flops=8 * samples * rows * block, bytes_accessed=8 * rows * block, transcendentals=0),
    )(where, weight, mod, xa, xb, total, grad)


def blank_kernel(out):
    pass


def ring_device(ring, x_first, x_layer, upstream, weight, bias):
    n = len(ring)
    half_way = n // 2
    block, samples = x_layer.shape
    half = block // 2
    parts = 2
    me = lax.axis_index("row")
    core = me % 2
    place = [0] * n
    for p, chip in enumerate(ring):
        place[chip] = p
    at = jnp.asarray(place, jnp.int32)[me // 2]
    order = jnp.asarray(ring, jnp.int32)

    def hop(by):
        return [(ring[p] * 2 + c, ring[(p + by) % n] * 2 + c) for p in range(n) for c in range(2)]

    swap = [(r, r ^ 1) for r in range(2 * n)]

    def send_up(v):
        return lax.ppermute(v, "row", hop(1))

    def send_down(v):
        return lax.ppermute(v, "row", hop(-1))

    def across(v):
        return lax.ppermute(v, "row", swap)

    def blocks_at(offset):
        chip = order[(at + offset + n) % n]
        return jnp.stack([chip * 2 + core, chip * 2 + 1 - core]).astype(jnp.int32)

    x_t = x_layer.T
    up_wide = upstream.astype(F32)
    mod_wide = lax.reduce_precision(up_wide * x_first.astype(F32), 8, 7)
    mod = mod_wide.astype(BF16)
    mod_t = mod.T
    bias_grad = jnp.sum(mod_wide, axis=1)

    held = {0: x_t}
    for s in range(1, half_way):
        held[-s] = send_up(held[1 - s])
        held[s] = send_down(held[s - 1])
    first = send_up(held[1 - half_way][:, :half])
    second = send_down(held[half_way - 1][:, half:])
    held[half_way] = jnp.concatenate([first, second], axis=1)

    offsets = [half_way]
    for s in range(half_way - 1, 0, -1):
        offsets += [s, -s]
    offsets.append(0)
    sums = {}
    for o in offsets:
        away, own = partials(blocks_at(o), mod_t, weight, block, parts)
        sums[o] = (own, across(away))

    def pair(o):
        own, other = sums[o]
        return own + other.astype(F32)

    far = pair(half_way)
    going_up = send_up(far[:, :half].astype(BF16))
    going_down = send_down(far[:, half:].astype(BF16))
    going_up = jnp.pad(going_up, ((0, 0), (0, block - half)))
    going_down = jnp.pad(going_down, ((0, 0), (half, 0)))
    for s in range(half_way - 1, 0, -1):
        going_up = send_up((pair(s) + going_up.astype(F32)).astype(BF16))
        going_down = send_down((pair(-s) + going_down.astype(F32)).astype(BF16))
    layer_grad = (pair(0) + going_up.astype(F32) + going_down.astype(F32)).astype(BF16).T

    rows = weight.shape[0]
    grad = pl.pallas_call(
        blank_kernel,
        out_specs=pl.BlockSpec(memory_space=pl.ANY),
        out_shape=jax.ShapeDtypeStruct(weight.shape, BF16),
    )()
    total = jnp.broadcast_to(bias[:, None], (rows, samples))
    for o in [0] + [sign * s for s in range(1, half_way) for sign in (-1, 1)] + [half_way]:
        total, grad = forward(blocks_at(o), weight, mod, held[o], across(held[o]), total, grad, parts)
    first_grad = (up_wide * total).astype(BF16)
    return (first_grad, layer_grad, grad, bias_grad)


def plain_device(x_first, x_layer, upstream, weight, bias):
    gathered = lax.all_gather(x_layer, "row", axis=0, tiled=True)
    affine = jnp.dot(weight, gathered, preferred_element_type=F32) + bias[:, None]
    up_wide = upstream.astype(F32)
    first_grad = (up_wide * affine).astype(BF16)
    modulated = (up_wide * x_first.astype(F32)).astype(BF16)
    weight_grad = lax.dot_general(modulated, gathered, (((1,), (1,)), ((), ())), preferred_element_type=F32).astype(BF16)
    bias_grad = jnp.sum(modulated.astype(F32), axis=1)
    share = lax.dot_general(weight, modulated, (((0,), (0,)), ((), ())), preferred_element_type=F32)
    layer_grad = lax.psum_scatter(share, "row", scatter_dimension=0, tiled=True).astype(BF16)
    return (first_grad, layer_grad, weight_grad, bias_grad)


def solution(mesh):
    chips = mesh.shape["row"] // 2
    on_device = functools.partial(ring_device, ring_of(chips)) if chips <= 16 else plain_device
    in_specs = (P("row", "group"), P("row", "group"), P("row", "group"), P("row", None), P("row"))
    out_specs = (
        P("row", "group"),
        P("row", "group"),
        P(("group", "row"), None),
        P(("group", "row")),
    )
    return jax.shard_map(
        on_device, mesh=mesh, in_specs=in_specs, out_specs=out_specs, check_vma=False
    )
```

```python
import functools

import jax
import jax.numpy as jnp
from jax import lax
from jax.experimental import pallas as pl
from jax.experimental.pallas import tpu as pltpu
from jax.sharding import PartitionSpec as P

F32 = jnp.float32
BF16 = jnp.bfloat16


def ring_of(n):
    width = {8: 2, 64: 4}.get(n, 2)
    depth = n // width
    walk = []
    for z in range(depth):
        xs = list(range(1, width))
        walk += [z * width + x for x in (xs if z % 2 == 0 else xs[::-1])]
    return walk + [z * width for z in reversed(range(depth))]


ANYWHERE = pl.BlockSpec(memory_space=pl.ANY)


TOKEN = jax.ShapeDtypeStruct((8, 128), F32)


def partial_kernel(k, where, mod_t, w, *refs):
    away, own = refs[-3:-1]
    t = pl.program_id(0)
    out = jnp.dot(mod_t[...], w[...], preferred_element_type=F32)

    @pl.when(t < k)
    def _():
        away[...] = out.astype(away.dtype)

    @pl.when(t >= k)
    def _():
        own[...] = out


def partials(where, base, k, mod_t, weight, block, after):
    samples, rows = mod_t.shape
    return pl.pallas_call(
        functools.partial(partial_kernel, k),
        grid_spec=pltpu.PrefetchScalarGridSpec(
            num_scalar_prefetch=1,
            grid=(2 * k,),
            in_specs=[
                pl.BlockSpec((samples, rows), lambda t, s: (0, 0)),
                pl.BlockSpec((rows, block), lambda t, s: (0, s[base + t])),
            ]
            + [ANYWHERE] * len(after),
            out_specs=[
                pl.BlockSpec((None, samples, block), lambda t, s: (jnp.minimum(t, k - 1), 0, 0)),
                pl.BlockSpec((None, samples, block), lambda t, s: (jnp.maximum(t - k, 0), 0, 0)),
                ANYWHERE,
            ],
        ),
        out_shape=[jax.ShapeDtypeStruct((k, samples, block), BF16), jax.ShapeDtypeStruct((k, samples, block), F32), TOKEN],
        compiler_params=pltpu.CompilerParams(vmem_limit_bytes=24 << 20),
        cost_estimate=pl.CostEstimate(
            flops=4 * k * samples * rows * block, bytes_accessed=4 * k * rows * block, transcendentals=0
        ),
    )(where, mod_t, weight, *after)


def forward_kernel(k, chained, where, w, mod, *refs):
    xs, (total, grad) = refs[:k], refs[-3:-1]
    t = pl.program_id(0)

    @pl.when(t == 0)
    def _():
        total[...] = refs[k][...] if chained else jnp.zeros_like(total)

    def step(x):
        total[...] += lax.dot_general(x[...], w[...], (((1,), (1,)), ((), ())), preferred_element_type=F32)
        grad[...] = jnp.dot(mod[...], x[...], preferred_element_type=F32).astype(grad.dtype)

    for i in range(k):
        pl.when(t == i)(functools.partial(step, xs[i]))


def forward(where, base, weight, mod, xs, carry, after):
    rows, samples = mod.shape
    block = xs[0].shape[1]
    k = len(xs)
    whole = pl.BlockSpec((samples, rows), lambda t, s: (0, 0))
    column = pl.BlockSpec((rows, block), lambda t, s: (0, s[base + t]))
    return pl.pallas_call(
        functools.partial(forward_kernel, k, bool(carry)),
        grid_spec=pltpu.PrefetchScalarGridSpec(
            num_scalar_prefetch=1,
            grid=(k,),
            in_specs=[column, pl.BlockSpec((rows, samples), lambda t, s: (0, 0))]
            + [pl.BlockSpec((samples, block), lambda t, s: (0, 0))] * k
            + ([whole, ANYWHERE] if carry else [])
            + [ANYWHERE] * len(after),
            out_specs=[whole, column, ANYWHERE],
        ),
        out_shape=[jax.ShapeDtypeStruct((samples, rows), F32), jax.ShapeDtypeStruct(weight.shape, BF16), TOKEN],
        input_output_aliases={3 + k: 0, 4 + k: 1} if carry else {},
        compiler_params=pltpu.CompilerParams(vmem_limit_bytes=40 << 20),
        cost_estimate=pl.CostEstimate(
            flops=4 * k * samples * rows * block, bytes_accessed=4 * k * rows * block, transcendentals=0
        ),
    )(where, weight, mod, *xs, *carry, *after)


def ring_device(ring, x_first, x_layer, upstream, weight, bias):
    n = len(ring)
    far = n // 2
    block = x_layer.shape[0]
    half = block // 2

    def hop(by):
        return [(ring[p] * 2 + c, ring[(p + by) % n] * 2 + c) for p in range(n) for c in range(2)]

    swap = [(r, r ^ 1) for r in range(2 * n)]

    def send_up(v):
        return lax.ppermute(v, "row", hop(1))

    def send_down(v):
        return lax.ppermute(v, "row", hop(-1))

    def across(v):
        return lax.ppermute(v, "row", swap)

    near = [[0, -1, 1]] + [[-s, s] for s in range(2, far)] + [[far]]
    outer = [[far, far - 1, 1 - far]] + [[2, -2, 1], [-1, 0]]
    table, bases, fill = [], {}, 0
    for name, group in [("p%d" % i, g) for i, g in enumerate(outer)] + [("f%d" % i, g) for i, g in enumerate(near)]:
        bases[name] = fill
        fill += 2 * len(group)
    for r in range(2 * n):
        p, core = ring.index(r // 2), r % 2
        line = []
        for group in outer:
            chips = [ring[(p + o) % n] for o in group]
            line += [chip * 2 + 1 - core for chip in chips] + [chip * 2 + core for chip in chips]
        for group in near:
            for o in group:
                chip = ring[(p + o) % n]
                line += [chip * 2 + core, chip * 2 + 1 - core]
        table.append(line)
    where = jnp.asarray(table, jnp.int32)[lax.axis_index("row")]

    x_t = x_layer.T
    up_t = upstream.T.astype(F32)
    mod_wide = lax.reduce_precision(up_t * x_first.T.astype(F32), 8, 7)
    mod_t = mod_wide.astype(BF16)
    mod = mod_t.T
    bias_grad = jnp.sum(mod_wide, axis=0)

    held, other = {0: x_t}, {0: across(x_t)}
    sums = {}

    def gather_step(s):
        up, down = held[1 - s], held[s - 1]
        if s == far:
            up, down = up[:, :half], down[:, half:]
        return [send_up(up), send_down(down)]

    def gathered(s, arrived):
        if s == far:
            held[far] = jnp.concatenate(arrived, axis=1)
            other[far] = across(held[far])
        else:
            held[-s], held[s] = arrived
            other[-s], other[s] = across(held[-s]), across(held[s])

    def share(i, away, own):
        back = across(away)
        for j, o in enumerate(outer[i]):
            sums[o] = (own, back, j)
        return back

    def partial_group(i, after):
        return partials(where, bases["p%d" % i], len(outer[i]), mod_t, weight, block, after)

    def pair(o):
        own, back, j = sums[o]
        return own[j] + back[j].astype(F32)

    def forward_group(i, carry, after):
        xs = [v for o in near[i] for v in (held[o], other[o])]
        return forward(where, bases["f%d" % i], weight, mod, xs, carry, after)

    def reduce_step(s, ups, downs):
        if s == far:
            both = pair(far)
            ups = send_up(both[:, :half].astype(BF16))
            downs = send_down(both[:, half:].astype(BF16))
        elif s == far - 1:
            ups = jnp.pad(ups, ((0, 0), (0, block - half)))
            downs = jnp.pad(downs, ((0, 0), (half, 0)))
            ups = send_up((pair(s) + ups.astype(F32)).astype(BF16))
            downs = send_down((pair(-s) + downs.astype(F32)).astype(BF16))
        else:
            ups = send_up((pair(s) + ups.astype(F32)).astype(BF16))
            downs = send_down((pair(-s) + downs.astype(F32)).astype(BF16))
        return ups, downs

    first = gather_step(1)
    away, own, _ = partial_group(0, [])
    away, *first = lax.optimization_barrier((away, *first))
    gathered(1, first)
    back = share(0, away, own)
    second = gather_step(2)
    away, own, token = partial_group(1, first)
    *second, token = lax.optimization_barrier((*second, token))
    share(1, away, own)
    gathered(2, second)
    third = gather_step(3)
    ups, downs = reduce_step(4, None, None)
    away, own, later = partial_group(2, [*second, back, token])
    share(2, away, own)
    *third, later = lax.optimization_barrier((*third, later))
    gathered(3, third)
    fourth = gather_step(4)
    ups, downs = reduce_step(3, ups, downs)
    *carry, token = forward_group(0, [], [*third, later])
    gathered(4, fourth)
    *carry, _ = forward_group(1, carry, [*fourth, ups, downs])
    ups, downs = reduce_step(2, ups, downs)
    *carry, _ = forward_group(2, carry, [ups, downs])
    ups, downs = reduce_step(1, ups, downs)
    *carry, _ = forward_group(3, carry, [])
    layer_grad = (pair(0) + ups.astype(F32) + downs.astype(F32)).astype(BF16).T
    total, grad = carry
    first_grad = (up_t * (total + bias[None, :])).astype(BF16).T
    return (first_grad, layer_grad, grad, bias_grad)


def plain_device(x_first, x_layer, upstream, weight, bias):
    gathered = lax.all_gather(x_layer, "row", axis=0, tiled=True)
    affine = jnp.dot(weight, gathered, preferred_element_type=F32) + bias[:, None]
    up_wide = upstream.astype(F32)
    first_grad = (up_wide * affine).astype(BF16)
    modulated = (up_wide * x_first.astype(F32)).astype(BF16)
    weight_grad = lax.dot_general(modulated, gathered, (((1,), (1,)), ((), ())), preferred_element_type=F32).astype(BF16)
    bias_grad = jnp.sum(modulated.astype(F32), axis=1)
    share = lax.dot_general(weight, modulated, (((0,), (0,)), ((), ())), preferred_element_type=F32)
    layer_grad = lax.psum_scatter(share, "row", scatter_dimension=0, tiled=True).astype(BF16)
    return (first_grad, layer_grad, weight_grad, bias_grad)


def solution(mesh):
    chips = mesh.shape["row"] // 2
    on_device = functools.partial(ring_device, ring_of(chips)) if chips == 8 else plain_device
    in_specs = (P("row", "group"), P("row", "group"), P("row", "group"), P("row", None), P("row"))
    out_specs = (
        P("row", "group"),
        P("row", "group"),
        P(("group", "row"), None),
        P(("group", "row")),
    )
    return jax.shard_map(
        on_device, mesh=mesh, in_specs=in_specs, out_specs=out_specs, check_vma=False
    )
```
